32 devices in a mesh: pole: 2 (over y), row: 4 (over z), col: 2 (over x), sub: 2 (over core).
Axes of the slice: x: 2, y: 2, z: 4, core: 2. Of those that a mesh axis runs over, the one named last changes fastest.
Arguments:
- sep_inverse: bfloat16 [8192, 4096], P(('pole', 'row', 'sub'), 'col'), parts along dimension 0, as said below
- parent_panel: bfloat16 [4, 4096, 1024], P(('pole', 'sub'), 'col'), parts along dimension 0, may hold values from -0.09375 to 0.09375
- parent_pivot: float32 [4, 1024, 1024], P(('pole', 'sub'), None, 'col'), parts along dimension 0, as said below
- parent_cols: int32 [2], replicated, may hold values from 1 to 8, as said below
- parent_blocks: int32 [2, 32], replicated, may hold values 0 or 1
- child_separator: bfloat16 [32, 1024, 512], P(('pole', 'row', 'sub'), 'col'), parts along dimension 0, may hold values from -0.1875 to 0.1875
- child_parent: bfloat16 [32, 1024, 512], P(('pole', 'row', 'sub'), 'col'), parts along dimension 0, may hold values from -0.1875 to 0.1875
- child_pivot: float32 [32, 512, 512], P(('pole', 'row', 'sub'), 'col'), parts along dimension 0, as said below
- child_cols: int32 [16], replicated, may hold values from 1 to 4, as said below
- child_blocks: int32 [16, 8], replicated, may hold values from 0 to 31, as said below
Outputs:
- parent_inverse: float32 [4, 1024, 1024], P(('pole', 'sub'), None, 'col'), parts along dimension 0
- parent_upper: float32 [4, 1024, 4096], P(('pole', 'sub'), 'col', 'row'), parts along dimension 0
- child_inverse: float32 [32, 512, 512], P(('pole', 'row', 'sub'), 'col'), parts along dimension 0
The draws below stay inside these ranges and needn't reach their ends.
There are 2 independent parts, one for each index of `pole`. The reference program is written for one: setup_inputs(seed, part) draws one part's arguments, and reference() takes and returns one part's arrays. A program takes and returns all parts, laid end to end along the dimension named above; an argument that names none is the same for every part. Nothing has to cross between parts.
Inputs may be any that keep to these rules, and one draw needn't show every extreme that they name: `parent_cols`: widths of the first-level supernodes in blocks of 128 columns; some supernode has 8. `child_cols`: widths of the second-level supernodes in blocks of 128 columns; some supernode has 4. `child_blocks`: each row holds 8 distinct block numbers in increasing order. `sep_inverse`: symmetric. `parent_pivot`: each block symmetric. `child_pivot`: each block symmetric.
All inputs are finite; a program needn't handle non-finite values.
Results may differ from the reference program's by a relative error of at most 0.0019.
Values may be sent and summed in bfloat16 or wider, within the bound.
A program may use at most 128 MiB of HBM per device.

```python
import math
import jax
import jax.numpy as jnp
from jax import lax

BLK = 128
NA = 4096
W1 = 1024
W2 = 512
P2A = 8
CHILD = 2
KIDS = 16
NBA = 32
NB1 = 8
NB2 = 4
N_SUB = 2


def shaped(noise_draw, diagonal, spread, order):
    symmetric = spread * (noise_draw + jnp.swapaxes(noise_draw, -1, -2)) / math.sqrt(2.0 * order)
    identity = jnp.eye(order, dtype=jnp.float32)
    matrix = symmetric + identity * diagonal[..., None, :]
    return matrix


def draw_sep_inverse(key, part):
    key = jax.random.fold_in(key, 11)
    key_noise, key_diag = jax.random.split(key, 2)
    diagonal = jax.random.uniform(key_diag, (NA,), jnp.float32, 0.5, 1.5)
    noise_draw = jax.random.normal(key_noise, (NA, NA), jnp.float32)
    return shaped(noise_draw, diagonal, 0.5, NA).astype(jnp.bfloat16)


def draw_parent_pivot(key, part):
    key = jax.random.fold_in(key, 12)
    key_noise, key_diag = jax.random.split(key, 2)
    diagonal = jax.random.uniform(key_diag, (N_SUB, W1), jnp.float32, 0.5, 1.5)
    noise_draw = jax.random.normal(key_noise, (N_SUB, W1, W1), jnp.float32)
    return shaped(noise_draw, diagonal, 2.0, W1)


def draw_child_pivot(key, part):
    key = jax.random.fold_in(key, 13)
    key_noise, key_diag = jax.random.split(key, 2)
    diagonal = jax.random.uniform(key_diag, (KIDS, W2), jnp.float32, 0.5, 1.5)
    noise_draw = jax.random.normal(key_noise, (KIDS, W2, W2), jnp.float32)
    return shaped(noise_draw, diagonal, 2.0, W2)


def sizes_with_top(key, number, largest):
    key_values, key_spot = jax.random.split(key)
    values = jax.random.randint(key_values, (number,), 1, largest + 1)
    spot_at = jax.random.randint(key_spot, (), 0, number)
    return values.at[spot_at].set(largest).astype(jnp.int32)


def draw_parent_cols(key, part):
    key = jax.random.fold_in(key, 21)
    return sizes_with_top(key, N_SUB, NB1)


def draw_child_cols(key, part):
    key = jax.random.fold_in(key, 22)
    return sizes_with_top(key, KIDS, NB2)


def draw_child_blocks(key, part):
    key = jax.random.fold_in(key, 23)
    child_keys = jax.random.split(key, KIDS)

    def pick_blocks(sub_key):
        shuffled = jax.random.permutation(sub_key, NBA)
        return jnp.sort(shuffled[:P2A])
    return jax.vmap(pick_blocks)(child_keys).astype(jnp.int32)


def plant(array, rng, smallest, high):
    spot = [jax.random.randint(jax.random.fold_in(rng, axis), (), 0, length) for axis, length in enumerate(array.shape)]
    main_axis = array.shape.index(max(array.shape))
    beside = spot[:main_axis] + [(spot[main_axis] + 1) % array.shape[main_axis]] + spot[main_axis + 1:]
    return array.at[tuple(spot)].set(smallest).at[tuple(beside)].set(high)


def steps_of(stream_key, shape, cuts, least, top_value):
    gain, own = 1.0, jax.random.fold_in(stream_key, 6)
    for dim, blocks in cuts:
        draws = jnp.exp(jax.random.uniform(jax.random.fold_in(own, dim), (blocks,), jnp.float32, least / len(cuts), top_value / len(cuts)))
        gain = gain * jnp.repeat(draws, shape[dim] // blocks).reshape([-1 if axis == dim else 1 for axis in range(len(shape))])
    return gain


def gaussian(own_key, shape, width, bound, pieces=(), kind=jnp.bfloat16):
    result = jax.random.normal(own_key, shape, jnp.float32) * width
    if len(pieces) > 0:
        result = steps_of(own_key, shape, pieces, -0.22, 0.18) * result
    return jnp.clip(result, min=-bound, max=bound).astype(kind)


def setup_inputs(seed: int = 0, part: int = 0) -> dict:
    arg_keys = jax.random.split(jax.random.key(seed), 11)
    part_splits = jax.random.split(jax.random.fold_in(arg_keys[10], part), 11)
    sep_inverse = draw_sep_inverse(jax.random.fold_in(jax.random.fold_in(arg_keys[10], part), 71), part)
    parent_panel = gaussian(part_splits[1], (N_SUB, NA, W1), NA ** -0.5, 0.09375, ((0, 2), (1, 2)))
    parent_pivot = draw_parent_pivot(jax.random.fold_in(jax.random.fold_in(arg_keys[10], part), 71), part)
    parent_cols = draw_parent_cols(jax.random.fold_in(arg_keys[10], 71), part)
    parent_blocks = plant((jax.random.randint(arg_keys[4], (N_SUB, NBA), 0, 4) < 3).astype(jnp.int32), jax.random.fold_in(arg_keys[4], 1), 0, 1)
    child_separator = gaussian(part_splits[5], (KIDS, P2A * BLK, W2), (P2A * BLK) ** -0.5, 0.1875, ((0, 8), (1, 2)))
    child_parent = gaussian(part_splits[6], (KIDS, W1, W2), W1 ** -0.5, 0.1875, ((0, 8), (1, 2)))
    child_pivot = draw_child_pivot(jax.random.fold_in(jax.random.fold_in(arg_keys[10], part), 71), part)
    child_cols = draw_child_cols(jax.random.fold_in(arg_keys[10], 71), part)
    child_blocks = draw_child_blocks(jax.random.fold_in(arg_keys[10], 71), part)
    return dict(sep_inverse=sep_inverse, parent_panel=parent_panel, parent_pivot=parent_pivot, parent_cols=parent_cols, parent_blocks=parent_blocks, child_separator=child_separator, child_parent=child_parent, child_pivot=child_pivot, child_cols=child_cols, child_blocks=child_blocks)


def as_float(value):
    return value.astype(jnp.float32)


def rounded(value):
    return lax.optimization_barrier(value.astype(jnp.bfloat16)).astype(jnp.float32)


def block_rows(blocks):
    return (blocks[:, None] * BLK + jnp.arange(BLK, dtype=jnp.int32)[None, :]).reshape(-1).astype(jnp.int32)


def reference(sep_inverse, parent_panel, parent_pivot, parent_cols, parent_blocks, child_separator, child_parent, child_pivot, child_cols, child_blocks):
    separator = as_float(sep_inverse)
    inverses = []
    uppers = []
    far_rounds = []
    inverse_rounds = []
    for branch in range(N_SUB):
        live_cols = jnp.arange(W1, dtype=jnp.int32) < parent_cols[branch] * BLK
        live_rows = jnp.repeat(parent_blocks[branch] > 0, BLK)
        panel_one = jnp.where(live_rows[:, None] & live_cols[None, :], as_float(parent_panel[branch]), jnp.float32(0.0))
        far_block = jnp.dot(separator, panel_one)
        far_round = rounded(far_block)
        pivot_block = jnp.where(live_cols[:, None] & live_cols[None, :], parent_pivot[branch], jnp.float32(0.0))
        inverse_block = pivot_block + jnp.dot(panel_one.T, far_round)
        inverses.append(inverse_block)
        uppers.append(-far_block.T)
        far_rounds.append(far_round)
        inverse_rounds.append(rounded(inverse_block))
    far_stack = jnp.stack(far_rounds)
    inverse_stack = jnp.stack(inverse_rounds)

    def one_child(child_index):
        branch = (child_index // CHILD) % N_SUB
        live_cols = jnp.arange(W2, dtype=jnp.int32) < child_cols[child_index] * BLK
        left_side = jnp.where(live_cols[None, :], as_float(child_separator[child_index]), jnp.float32(0.0))
        right_side = jnp.where(live_cols[None, :], as_float(child_parent[child_index]), jnp.float32(0.0))
        picked = block_rows(child_blocks[child_index])
        chosen = jnp.take(jnp.take(separator, picked, axis=0), picked, axis=1)
        left_sep = rounded(jnp.dot(left_side.T, chosen))
        left_cross = rounded(jnp.dot(left_side.T, jnp.take(far_stack[branch], picked, axis=0)))
        left_par = rounded(jnp.dot(right_side.T, inverse_stack[branch]))
        cross_term = jnp.dot(left_cross, right_side)
        pivot_block = jnp.where(live_cols[:, None] & live_cols[None, :], child_pivot[child_index], jnp.float32(0.0))
        return pivot_block + jnp.dot(left_sep, left_side) + jnp.dot(left_par, right_side) - cross_term - cross_term.T

    child_out = lax.map(one_child, jnp.arange(KIDS, dtype=jnp.int32))
    return jnp.stack(inverses), jnp.stack(uppers), child_out
```

```python
import jax
import jax.numpy as jnp
from jax import lax
from jax.sharding import PartitionSpec as P

BLK = 128
P2A = 8
CHILD = 2
BF = jnp.bfloat16
F32 = jnp.float32


def swap(value, axis):
    return lax.ppermute(value, axis, [(0, 1), (1, 0)])


def spread_2(value, axis, source):
    kept = jnp.where(lax.axis_index(axis) == source, value, 0).astype(value.dtype)
    return lax.psum(kept, axis)


def pair_gather(value, axis, dim):
    if lax.axis_size(axis) != 2:
        return lax.all_gather(value, axis, axis=dim, tiled=True)
    other = swap(value, axis)
    first = lax.axis_index(axis) == 0
    return jnp.concatenate(
        [jnp.where(first, value, other), jnp.where(first, other, value)], axis=dim
    )


def pair_scatter(value, axis):
    if lax.axis_size(axis) != 2:
        return lax.psum_scatter(value, axis, scatter_dimension=0, tiled=True)
    half = value.shape[0] // 2
    at = lax.axis_index(axis)
    sent = lax.dynamic_slice_in_dim(value, (1 - at) * half, half, 0)
    kept = lax.dynamic_slice_in_dim(value, at * half, half, 0)
    return kept + swap(sent, axis)


def dot(a, b, dims):
    return lax.dot_general(a, b, (dims, ((), ())), preferred_element_type=F32)


def per_device(
    sep_inverse,
    parent_panel,
    parent_pivot,
    parent_cols,
    parent_blocks,
    child_separator,
    child_parent,
    child_pivot,
    child_cols,
    child_blocks,
):
    rows_count = lax.axis_size("row")
    cols_count = lax.axis_size("col")
    subs_count = lax.axis_size("sub")
    row_at = lax.axis_index("row")
    col_at = lax.axis_index("col")
    sub_at = lax.axis_index("sub")
    strip_len = sep_inverse.shape[1]
    order = strip_len * cols_count
    band_len = order // rows_count
    w1 = parent_panel.shape[2]
    w2 = child_separator.shape[2]
    slice_one = w1 // cols_count
    slice_two = w2 // cols_count
    zero = jnp.zeros((), BF)

    whole_strip = lax.all_gather(sep_inverse, ("row", "sub"), axis=0, tiled=True)
    own_rows = pair_gather(sep_inverse, "sub", 0)

    count_one = lax.dynamic_index_in_dim(parent_cols, sub_at, 0, keepdims=False)
    blocks_one = lax.dynamic_index_in_dim(parent_blocks, sub_at, 0, keepdims=False)
    live_rows = jnp.broadcast_to(blocks_one[:, None] > 0, (order // BLK, BLK)).reshape(order)
    strip_live = lax.dynamic_slice_in_dim(live_rows, col_at * strip_len, strip_len, 0)
    live_one = jnp.arange(w1, dtype=jnp.int32) < count_one * BLK
    panel_one = jnp.where(strip_live[:, None] & live_one[None, :], parent_panel[0], zero)

    root_col = row_at * cols_count // rows_count
    offset = jnp.clip(row_at * band_len - root_col * strip_len, 0, strip_len - band_len)
    sent_rows = lax.dynamic_slice_in_dim(panel_one, offset, band_len, 0)
    if cols_count == 2:
        mine_rows = jnp.where(col_at == root_col, sent_rows, swap(sent_rows, "col"))
    else:
        mine_rows = spread_2(sent_rows, "col", root_col)
    far_block = pair_scatter(dot(panel_one, own_rows, ((0,), (1,))), "col")
    far_round = far_block.astype(BF)
    partial_value = dot(mine_rows, far_round, ((0,), (1,)))
    summed = lax.psum(partial_value, "row")
    keep_cols = lax.dynamic_slice_in_dim(live_one, col_at * slice_one, slice_one, 0)
    pivot_one = jnp.where(live_one[:, None] & keep_cols[None, :], parent_pivot[0], F32(0.0))
    inverse_one = pivot_one + summed
    inverse_round = inverse_one.astype(BF)

    side_rows = pair_gather(child_separator, "col", 1)
    upper_rows = pair_gather(child_parent, "col", 1)
    first_kid = (row_at * subs_count + sub_at) * CHILD
    kid_cols = lax.dynamic_slice_in_dim(child_cols, first_kid, CHILD, 0)
    kid_blocks = lax.dynamic_slice_in_dim(child_blocks, first_kid, CHILD, 0)
    live_two = jnp.arange(w2, dtype=jnp.int32)[None, :] < kid_cols[:, None] * BLK
    left_side = jnp.where(live_two[:, None, :], side_rows, zero)
    right_side = jnp.where(live_two[:, None, :], upper_rows, zero)
    strip_blocks = col_at * (strip_len // BLK) + jnp.arange(strip_len // BLK, dtype=jnp.int32)
    block_hits = (kid_blocks[:, None, :] == strip_blocks[None, :, None]).astype(BF)
    spread = jnp.einsum(
        "kbp,kpiw->kbiw",
        block_hits,
        left_side.reshape(CHILD, P2A, BLK, w2),
        preferred_element_type=F32,
    )
    spread = spread.astype(BF).reshape(CHILD, strip_len, w2)

    picked_rows = (
        kid_blocks[:, :, None] * BLK + jnp.arange(BLK, dtype=jnp.int32)[None, None, :]
    ).reshape(CHILD, P2A * BLK)

    terms = []
    for k in range(CHILD):
        right_slice = lax.dynamic_slice_in_dim(right_side[k], col_at * slice_one, slice_one, 0)
        left_par = dot(right_side[k], inverse_round, ((0,), (0,))).astype(BF)
        par_term = dot(left_par, right_slice, ((1,), (0,)))
        reach = dot(panel_one, right_side[k], ((1,), (0,))).astype(BF)
        chosen = jnp.take(whole_strip, picked_rows[k], axis=0)
        weight = dot(left_side[k], chosen, ((0,), (0,))).astype(BF)
        sep_term = dot(weight, spread[k], ((1,), (0,)))
        cross = dot(weight, reach, ((1,), (0,)))
        terms.append(sep_term + par_term - cross - cross.T)
    term_sum = jnp.stack(terms, axis=1)
    summed_two = pair_scatter(term_sum, "col")
    keep_two = lax.dynamic_slice_in_dim(live_two, col_at * slice_two, slice_two, 1)
    pivot_two = jnp.where(keep_two[:, :, None] & live_two[:, None, :], child_pivot, F32(0.0))
    child_out = pivot_two + jnp.transpose(summed_two, (1, 0, 2))
    return (inverse_one[None], (-far_block)[None], child_out)


def solution(mesh):
    return jax.shard_map(
        per_device,
        mesh=mesh,
        in_specs=(
            P(("pole", "row", "sub"), "col"),
            P(("pole", "sub"), "col", None),
            P(("pole", "sub"), None, "col"),
            P(),
            P(),
            P(("pole", "row", "sub"), "col", None),
            P(("pole", "row", "sub"), "col", None),
            P(("pole", "row", "sub"), "col", None),
            P(),
            P(),
        ),
        out_specs=(
            P(("pole", "sub"), None, "col"),
            P(("pole", "sub"), "col", "row"),
            P(("pole", "row", "sub"), "col", None),
        ),
        check_vma=False,
    )
```

```python
import functools

import jax
import jax.numpy as jnp
from jax import lax
from jax.experimental import pallas as pl
from jax.experimental.pallas import tpu as pltpu
from jax.sharding import PartitionSpec as P

BLK = 128
P2A = 8
CHILD = 2
BF = jnp.bfloat16
F32 = jnp.float32
MESH = pl.DeviceIdType.MESH


def swap(value, axis):
    return lax.ppermute(value, axis, [(0, 1), (1, 0)])


def spread_2(value, axis, source):
    kept = jnp.where(lax.axis_index(axis) == source, value, 0).astype(value.dtype)
    return lax.psum(kept, axis)


def pair_gather(value, axis, dim):
    if lax.axis_size(axis) != 2:
        return lax.all_gather(value, axis, axis=dim, tiled=True)
    other = swap(value, axis)
    first = lax.axis_index(axis) == 0
    return jnp.concatenate(
        [jnp.where(first, value, other), jnp.where(first, other, value)], axis=dim
    )


def pair_scatter(value, axis):
    if lax.axis_size(axis) != 2:
        return lax.psum_scatter(value, axis, scatter_dimension=0, tiled=True)
    half = value.shape[0] // 2
    at = lax.axis_index(axis)
    sent = lax.dynamic_slice_in_dim(value, (1 - at) * half, half, 0)
    kept = lax.dynamic_slice_in_dim(value, at * half, half, 0)
    return kept + swap(sent, axis)


def dot(a, b, dims):
    return lax.dot_general(a, b, (dims, ((), ())), preferred_element_type=F32)


def exchange_kernel(
    n,
    sep,
    panel,
    side,
    upper,
    strip,
    far,
    summed,
    side_full,
    upper_full,
    a_own,
    a_peer,
    p_send,
    p_recv,
    band,
    far_low,
    m_part,
    m_recv,
    total,
    up_sem,
    down_sem,
    row_sem,
    sub_send,
    sub_recv,
    x_send,
    x_recv,
    band_sem,
    kid_send,
    kid_recv,
    m_send,
    m_got,
    g_send,
    g_got,
    local_sem,
):
    z = lax.axis_index("row")
    c = lax.axis_index("col")
    s = lax.axis_index("sub")
    rows = sep.shape[0]
    half = far.shape[1]
    kid_rows = side.shape[1]
    band_len = band.shape[0]
    part = m_recv.shape[1]
    sub_peer = {"sub": 1 - s}
    col_peer = {"col": 1 - c}
    root = z * 2 // n
    base = pl.multiple_of((z - root * (n // 2)) * band_len, band_len)

    barrier = pltpu.get_barrier_semaphore()
    pl.semaphore_signal(barrier, inc=1, device_id=sub_peer, device_id_type=MESH)
    pl.semaphore_signal(barrier, inc=1, device_id=col_peer, device_id_type=MESH)
    for d in range(1, n):
        pl.semaphore_signal(
            barrier, inc=1, device_id={"row": lax.rem(z + d, n)}, device_id_type=MESH
        )
    pl.semaphore_wait(barrier, n + 1)

    def piece(p, sub):
        return strip.at[pl.ds(pl.multiple_of((p * 2 + sub) * rows, rows), rows), :]

    def remote(src, dst, send, recv, to):
        return pltpu.make_async_remote_copy(
            src_ref=src, dst_ref=dst, send_sem=send, recv_sem=recv, device_id=to, device_id_type=MESH
        )

    def up(t, p, src):
        return remote(src, piece(p, s), up_sem.at[t], row_sem.at[p], {"row": z + 1})

    def down(t, p, src):
        return remote(src, piece(p, s), down_sem.at[t], row_sem.at[p], {"row": z - 1})

    def across(p, src):
        return remote(src, piece(p, s), sub_send.at[p], sub_recv.at[p], sub_peer)

    def from_peer(p):
        return remote(piece(p, 1 - s), piece(p, 1 - s), sub_send.at[p], sub_recv.at[p], sub_peer)

    def far_copy(j):
        at = pl.ds(pl.multiple_of(j * rows, rows), rows)
        return remote(p_send.at[at, :], p_recv.at[at, :], x_send.at[j], x_recv.at[j], col_peer)

    def kid_copy(i):
        src, dst = ((side, side_full), (upper, upper_full))[i]
        place = dst.at[:, pl.ds(pl.multiple_of(c * kid_rows, kid_rows), kid_rows), :]
        return remote(src, place, kid_send.at[i], kid_recv.at[i], col_peer)

    def kid_own(i):
        src, dst = ((side, side_full), (upper, upper_full))[i]
        place = dst.at[:, pl.ds(pl.multiple_of(c * kid_rows, kid_rows), kid_rows), :]
        return pltpu.make_async_copy(src, place, local_sem.at[4 + i])

    def quarter(q):
        return pl.ds(pl.multiple_of(q * part, part), part)

    def m_copy(q):
        return remote(
            m_part.at[quarter(q), :], m_recv.at[z], m_send.at[q], m_got.at[z], {"row": q}
        )

    def m_from(p):
        return remote(m_part.at[quarter(p), :], m_recv.at[p], m_send.at[p], m_got.at[p], {"row": p})

    def g_copy(q):
        return remote(total, summed.at[quarter(z), :], g_send.at[q], g_got.at[z], {"row": q})

    def g_from(p):
        return remote(total, summed.at[quarter(p), :], g_send.at[p], g_got.at[p], {"row": p})

    load = pltpu.make_async_copy(sep, a_own, local_sem.at[0])
    load.start()

    @pl.when(z + 1 < n)
    def _():
        up(0, z, sep).start()

    @pl.when(z >= 1)
    def _():
        down(0, z, sep).start()

    across(z, sep).start()
    own = pltpu.make_async_copy(sep, piece(z, s), local_sem.at[1])
    own.start()
    band_out = remote(
        panel.at[pl.ds(base, band_len), :], band, band_sem.at[0], band_sem.at[1], col_peer
    )
    band_own = pltpu.make_async_copy(panel.at[pl.ds(base, band_len), :], band, local_sem.at[2])

    @pl.when(c == root)
    def _():
        band_own.start()

    tile = min(256, rows)
    theirs = pl.ds(pl.multiple_of((1 - c) * half, half), half)
    mine = pl.ds(pl.multiple_of(c * half, half), half)

    def partial(src, dst, first, columns):
        @pl.loop(0, rows // tile)
        def _(i):
            at = pl.ds(pl.multiple_of(i * tile, tile), tile)
            to = pl.ds(pl.multiple_of(first * rows + i * tile, tile), tile)
            dst[to, :] = jnp.dot(src[at, :], panel[:, columns], preferred_element_type=F32)

    load.wait()
    partial(a_own, p_send, s, theirs)
    far_copy(s).start()

    from_peer(z).wait_recv()
    fetch = pltpu.make_async_copy(piece(z, 1 - s), a_peer, local_sem.at[3])
    fetch.start()
    fetch.wait()
    partial(a_peer, p_send, 1 - s, theirs)
    far_copy(1 - s).start()

    @pl.when(c == root)
    def _():
        band_out.start()

    for i in range(2):
        kid_own(i).start()
    partial(a_own, far, s, mine)
    partial(a_peer, far, 1 - s, mine)

    def arrive(t):
        below, above = z - 1 - t, z + 1 + t

        @pl.when(below >= 0)
        def _():
            up(t, below, piece(below, s)).wait_recv()
            if t < n - 2:
                @pl.when(z + 1 < n)
                def _():
                    up(t + 1, below, piece(below, s)).start()
            across(below, piece(below, s)).start()

        @pl.when(above < n)
        def _():
            down(t, above, piece(above, s)).wait_recv()
            if t < n - 2:
                @pl.when(z >= 1)
                def _():
                    down(t + 1, above, piece(above, s)).start()
            across(above, piece(above, s)).start()

    arrive(0)

    for j in (s, 1 - s):
        far_copy(j).wait_recv()

        @pl.loop(0, rows // tile)
        def _(i):
            at = pl.ds(pl.multiple_of(j * rows + i * tile, tile), tile)
            value = far[at, :] + p_recv[at, :]
            far[at, :] = value
            far_low[at, :] = value.astype(BF)

    for i in range(2):
        kid_copy(i).start()

    @pl.when(c == root)
    def _():
        band_own.wait()
        band_out.wait_send()

    @pl.when(c != root)
    def _():
        band_out.wait_recv()

    @pl.loop(0, n)
    def _(q):
        m_part[quarter(q), :] = lax.dot_general(
            band[:, quarter(q)],
            far_low[...],
            (((0,), (0,)), ((), ())),
            preferred_element_type=F32,
        )

    others = [lax.rem(z + d, n) for d in range(1, n)]
    for q in others:
        m_copy(q).start()
    for t in range(1, n - 2):
        arrive(t)
    for p in others:
        m_from(p).wait_recv()
    value = m_part[quarter(z), :]
    for p in others:
        value = value + m_recv[p]
    total[...] = value
    for q in others:
        g_copy(q).start()
    keep = pltpu.make_async_copy(total, summed.at[quarter(z), :], local_sem.at[6])
    keep.start()
    arrive(n - 2)

    own.wait()
    keep.wait()
    for i in range(2):
        kid_own(i).wait()
        kid_copy(i).wait_send()
        kid_copy(i).wait_recv()
    for j in (s, 1 - s):
        far_copy(j).wait_send()
    for p in others:
        m_copy(p).wait_send()
        g_copy(p).wait_send()
        g_from(p).wait_recv()
        from_peer(p).wait_recv()
        across(p, piece(p, s)).wait_send()
    across(z, sep).wait_send()
    for t in range(n - 1):
        @pl.when((z - t >= 0) & (z + 1 < n))
        def _():
            up(t, z - t, piece(z, s)).wait_send()

        @pl.when((z + t < n) & (z >= 1))
        def _():
            down(t, z + t, piece(z, s)).wait_send()


def exchange(sep, panel, side, upper):
    n = lax.axis_size("row")
    rows, strip_len = sep.shape
    w1 = panel.shape[1]
    half = w1 // 2
    kids, kid_rows, w2 = side.shape
    band_len = 2 * rows
    part = w1 // n
    any_spec = pl.BlockSpec(memory_space=pl.ANY)
    vmem = pl.BlockSpec(memory_space=pltpu.VMEM)
    dma = pltpu.SemaphoreType.DMA
    full = jax.ShapeDtypeStruct((kids, 2 * kid_rows, w2), BF)
    return pl.pallas_call(
        functools.partial(exchange_kernel, n),
        out_shape=(
            jax.ShapeDtypeStruct((n * band_len, strip_len), BF),
            jax.ShapeDtypeStruct((band_len, half), F32),
            jax.ShapeDtypeStruct((w1, half), F32),
            full,
            full,
        ),
        in_specs=[any_spec, vmem, any_spec, any_spec],
        out_specs=(any_spec, vmem, any_spec, any_spec, any_spec),
        scratch_shapes=[
            pltpu.VMEM((rows, strip_len), BF),
            pltpu.VMEM((rows, strip_len), BF),
            pltpu.VMEM((band_len, half), F32),
            pltpu.VMEM((band_len, half), F32),
            pltpu.VMEM((band_len, w1), BF),
            pltpu.VMEM((band_len, half), BF),
            pltpu.VMEM((w1, half), F32),
            pltpu.VMEM((n, part, half), F32),
            pltpu.VMEM((part, half), F32),
            dma((n,)),
            dma((n,)),
            dma((n,)),
            dma((n,)),
            dma((n,)),
            dma((2,)),
            dma((2,)),
            dma((2,)),
            dma((2,)),
            dma((2,)),
            dma((n,)),
            dma((n,)),
            dma((n,)),
            dma((n,)),
            dma((8,)),
        ],
        compiler_params=pltpu.CompilerParams(
            collective_id=0, has_side_effects=True, vmem_limit_bytes=48 * 2**20
        ),
    )(sep, panel, side, upper)


def per_device(
    sep_inverse,
    parent_panel,
    parent_pivot,
    parent_cols,
    parent_blocks,
    child_separator,
    child_parent,
    child_pivot,
    child_cols,
    child_blocks,
):
    rows_count = lax.axis_size("row")
    cols_count = lax.axis_size("col")
    subs_count = lax.axis_size("sub")
    row_at = lax.axis_index("row")
    col_at = lax.axis_index("col")
    sub_at = lax.axis_index("sub")
    strip_len = sep_inverse.shape[1]
    order = strip_len * cols_count
    band_len = order // rows_count
    w1 = parent_panel.shape[2]
    w2 = child_separator.shape[2]
    slice_one = w1 // cols_count
    slice_two = w2 // cols_count
    zero = jnp.zeros((), BF)

    count_one = lax.dynamic_index_in_dim(parent_cols, sub_at, 0, keepdims=False)
    blocks_one = lax.dynamic_index_in_dim(parent_blocks, sub_at, 0, keepdims=False)
    live_rows = jnp.broadcast_to(blocks_one[:, None] > 0, (order // BLK, BLK)).reshape(order)
    strip_live = lax.dynamic_slice_in_dim(live_rows, col_at * strip_len, strip_len, 0)
    live_one = jnp.arange(w1, dtype=jnp.int32) < count_one * BLK
    panel_one = jnp.where(strip_live[:, None] & live_one[None, :], parent_panel[0], zero)

    if rows_count == 4 and cols_count == 2 and subs_count == 2:
        whole_strip, far_rows, summed, side_rows, upper_rows = exchange(
            sep_inverse, panel_one, child_separator, child_parent
        )
        far_block = far_rows.T
    else:
        whole_strip = lax.all_gather(sep_inverse, ("row", "sub"), axis=0, tiled=True)
        own_rows = pair_gather(sep_inverse, "sub", 0)
        root_col = row_at * cols_count // rows_count
        offset = jnp.clip(row_at * band_len - root_col * strip_len, 0, strip_len - band_len)
        sent_rows = lax.dynamic_slice_in_dim(panel_one, offset, band_len, 0)
        mine_rows = spread_2(sent_rows, "col", root_col)
        far_block = pair_scatter(dot(panel_one, own_rows, ((0,), (1,))), "col")
        far_round = far_block.astype(BF)
        partial_value = dot(mine_rows, far_round, ((0,), (1,)))
        summed = lax.psum(partial_value, "row")
        side_rows = pair_gather(child_separator, "col", 1)
        upper_rows = pair_gather(child_parent, "col", 1)
    keep_cols = lax.dynamic_slice_in_dim(live_one, col_at * slice_one, slice_one, 0)
    pivot_one = jnp.where(live_one[:, None] & keep_cols[None, :], parent_pivot[0], F32(0.0))
    inverse_one = pivot_one + summed
    inverse_round = inverse_one.astype(BF)

    first_kid = (row_at * subs_count + sub_at) * CHILD
    kid_cols = lax.dynamic_slice_in_dim(child_cols, first_kid, CHILD, 0)
    kid_blocks = lax.dynamic_slice_in_dim(child_blocks, first_kid, CHILD, 0)
    live_two = jnp.arange(w2, dtype=jnp.int32)[None, :] < kid_cols[:, None] * BLK
    left_side = jnp.where(live_two[:, None, :], side_rows, zero)
    right_side = jnp.where(live_two[:, None, :], upper_rows, zero)
    strip_blocks = col_at * (strip_len // BLK) + jnp.arange(strip_len // BLK, dtype=jnp.int32)
    block_hits = (kid_blocks[:, None, :] == strip_blocks[None, :, None]).astype(BF)
    spread = jnp.einsum(
        "kbp,kpiw->kbiw",
        block_hits,
        left_side.reshape(CHILD, P2A, BLK, w2),
        preferred_element_type=F32,
    )
    spread = spread.astype(BF).reshape(CHILD, strip_len, w2)

    picked_rows = (
        kid_blocks[:, :, None] * BLK + jnp.arange(BLK, dtype=jnp.int32)[None, None, :]
    ).reshape(CHILD, P2A * BLK)

    terms = []
    for k in range(CHILD):
        right_slice = lax.dynamic_slice_in_dim(right_side[k], col_at * slice_one, slice_one, 0)
        left_par = dot(right_side[k], inverse_round, ((0,), (0,))).astype(BF)
        par_term = dot(left_par, right_slice, ((1,), (0,)))
        reach = dot(panel_one, right_side[k], ((1,), (0,))).astype(BF)
        chosen = jnp.take(whole_strip, picked_rows[k], axis=0)
        weight = dot(left_side[k], chosen, ((0,), (0,))).astype(BF)
        sep_term = dot(weight, spread[k], ((1,), (0,)))
        cross = dot(weight, reach, ((1,), (0,)))
        terms.append(sep_term + par_term - cross - cross.T)
    term_sum = jnp.stack(terms, axis=1)
    summed_two = pair_scatter(term_sum, "col")
    keep_two = lax.dynamic_slice_in_dim(live_two, col_at * slice_two, slice_two, 1)
    pivot_two = jnp.where(keep_two[:, :, None] & live_two[:, None, :], child_pivot, F32(0.0))
    child_out = pivot_two + jnp.transpose(summed_two, (1, 0, 2))
    return (inverse_one[None], (-far_block)[None], child_out)


def solution(mesh):
    return jax.shard_map(
        per_device,
        mesh=mesh,
        in_specs=(
            P(("pole", "row", "sub"), "col"),
            P(("pole", "sub"), "col", None),
            P(("pole", "sub"), None, "col"),
            P(),
            P(),
            P(("pole", "row", "sub"), "col", None),
            P(("pole", "row", "sub"), "col", None),
            P(("pole", "row", "sub"), "col", None),
            P(),
            P(),
        ),
        out_specs=(
            P(("pole", "sub"), None, "col"),
            P(("pole", "sub"), "col", "row"),
            P(("pole", "row", "sub"), "col", None),
        ),
        check_vma=False,
    )
```

```python
import functools

import jax
import jax.numpy as jnp
from jax import lax
from jax.experimental import pallas as pl
from jax.experimental.pallas import tpu as pltpu
from jax.sharding import PartitionSpec as P

BLK = 128
P2A = 8
CHILD = 2
BF = jnp.bfloat16
F32 = jnp.float32
MESH = pl.DeviceIdType.MESH


def swap(value, axis):
    return lax.ppermute(value, axis, [(0, 1), (1, 0)])


def spread_2(value, axis, source):
    kept = jnp.where(lax.axis_index(axis) == source, value, 0).astype(value.dtype)
    return lax.psum(kept, axis)


def pair_gather(value, axis, dim):
    if lax.axis_size(axis) != 2:
        return lax.all_gather(value, axis, axis=dim, tiled=True)
    other = swap(value, axis)
    first = lax.axis_index(axis) == 0
    return jnp.concatenate(
        [jnp.where(first, value, other), jnp.where(first, other, value)], axis=dim
    )


def pair_scatter(value, axis, dim):
    if lax.axis_size(axis) != 2:
        return lax.psum_scatter(value, axis, scatter_dimension=dim, tiled=True)
    half = value.shape[dim] // 2
    at = lax.axis_index(axis)
    sent = lax.dynamic_slice_in_dim(value, (1 - at) * half, half, dim)
    kept = lax.dynamic_slice_in_dim(value, at * half, half, dim)
    return kept + swap(sent, axis)


def dot(a, b, dims):
    return lax.dot_general(a, b, (dims, ((), ())), preferred_element_type=F32)


def exchange_kernel(
    n,
    sep,
    panel,
    side,
    upper,
    strip,
    far,
    summed,
    side_full,
    upper_full,
    a_own,
    a_peer,
    p_send,
    p_recv,
    band,
    far_low,
    m_part,
    m_recv,
    total,
    up_sem,
    down_sem,
    row_sem,
    sub_send,
    sub_recv,
    x_send,
    x_recv,
    band_sem,
    kid_send,
    kid_recv,
    m_send,
    m_got,
    g_send,
    g_got,
    local_sem,
):
    z = lax.axis_index("row")
    c = lax.axis_index("col")
    s = lax.axis_index("sub")
    rows = sep.shape[0]
    half = far.shape[1]
    kid_rows = side.shape[1]
    band_len = band.shape[0]
    part = m_recv.shape[1]
    sub_peer = {"sub": 1 - s}
    col_peer = {"col": 1 - c}
    root = z * 2 // n
    base = pl.multiple_of((z - root * (n // 2)) * band_len, band_len)

    barrier = pltpu.get_barrier_semaphore()
    pl.semaphore_signal(barrier, inc=1, device_id=sub_peer, device_id_type=MESH)
    pl.semaphore_signal(barrier, inc=1, device_id=col_peer, device_id_type=MESH)
    for d in range(1, n):
        pl.semaphore_signal(
            barrier, inc=1, device_id={"row": lax.rem(z + d, n)}, device_id_type=MESH
        )
    pl.semaphore_wait(barrier, n + 1)

    def piece(p, sub):
        return strip.at[pl.ds(pl.multiple_of((p * 2 + sub) * rows, rows), rows), :]

    def remote(src, dst, send, recv, to):
        return pltpu.make_async_remote_copy(
            src_ref=src, dst_ref=dst, send_sem=send, recv_sem=recv, device_id=to, device_id_type=MESH
        )

    def up(t, p, src):
        return remote(src, piece(p, s), up_sem.at[t], row_sem.at[p], {"row": z + 1})

    def down(t, p, src):
        return remote(src, piece(p, s), down_sem.at[t], row_sem.at[p], {"row": z - 1})

    def across(p, src):
        return remote(src, piece(p, s), sub_send.at[p], sub_recv.at[p], sub_peer)

    def from_peer(p):
        return remote(piece(p, 1 - s), piece(p, 1 - s), sub_send.at[p], sub_recv.at[p], sub_peer)

    def far_copy(j):
        at = pl.ds(pl.multiple_of(j * rows, rows), rows)
        return remote(p_send.at[at, :], p_recv.at[at, :], x_send.at[j], x_recv.at[j], col_peer)

    def kid_copy(i):
        src, dst = ((side, side_full), (upper, upper_full))[i]
        place = dst.at[:, pl.ds(pl.multiple_of(c * kid_rows, kid_rows), kid_rows), :]
        return remote(src, place, kid_send.at[i], kid_recv.at[i], col_peer)

    def kid_own(i):
        src, dst = ((side, side_full), (upper, upper_full))[i]
        place = dst.at[:, pl.ds(pl.multiple_of(c * kid_rows, kid_rows), kid_rows), :]
        return pltpu.make_async_copy(src, place, local_sem.at[4 + i])

    def quarter(q):
        return pl.ds(pl.multiple_of(q * part, part), part)

    def m_copy(q):
        return remote(
            m_part.at[quarter(q), :], m_recv.at[z], m_send.at[q], m_got.at[z], {"row": q}
        )

    def m_from(p):
        return remote(m_part.at[quarter(p), :], m_recv.at[p], m_send.at[p], m_got.at[p], {"row": p})

    def g_copy(q):
        return remote(total, summed.at[quarter(z), :], g_send.at[q], g_got.at[z], {"row": q})

    def g_from(p):
        return remote(total, summed.at[quarter(p), :], g_send.at[p], g_got.at[p], {"row": p})

    load = pltpu.make_async_copy(sep, a_own, local_sem.at[0])
    load.start()

    @pl.when(z + 1 < n)
    def _():
        up(0, z, sep).start()

    @pl.when(z >= 1)
    def _():
        down(0, z, sep).start()

    across(z, sep).start()
    own = pltpu.make_async_copy(sep, piece(z, s), local_sem.at[1])
    own.start()
    band_out = remote(
        panel.at[pl.ds(base, band_len), :], band, band_sem.at[0], band_sem.at[1], col_peer
    )
    band_own = pltpu.make_async_copy(panel.at[pl.ds(base, band_len), :], band, local_sem.at[2])

    @pl.when(c == root)
    def _():
        band_own.start()

    tile = min(256, rows)
    theirs = pl.ds(pl.multiple_of((1 - c) * half, half), half)
    mine = pl.ds(pl.multiple_of(c * half, half), half)

    def partial(src, dst, first, columns):
        @pl.loop(0, rows // tile)
        def _(i):
            at = pl.ds(pl.multiple_of(i * tile, tile), tile)
            to = pl.ds(pl.multiple_of(first * rows + i * tile, tile), tile)
            dst[to, :] = jnp.dot(src[at, :], panel[:, columns], preferred_element_type=F32)

    load.wait()
    partial(a_own, p_send, s, theirs)
    far_copy(s).start()

    from_peer(z).wait_recv()
    fetch = pltpu.make_async_copy(piece(z, 1 - s), a_peer, local_sem.at[3])
    fetch.start()
    fetch.wait()
    partial(a_peer, p_send, 1 - s, theirs)
    far_copy(1 - s).start()

    @pl.when(c == root)
    def _():
        band_out.start()

    for i in range(2):
        kid_own(i).start()
    partial(a_own, far, s, mine)
    partial(a_peer, far, 1 - s, mine)

    def arrive(t):
        below, above = z - 1 - t, z + 1 + t

        @pl.when(below >= 0)
        def _():
            up(t, below, piece(below, s)).wait_recv()
            if t < n - 2:
                @pl.when(z + 1 < n)
                def _():
                    up(t + 1, below, piece(below, s)).start()
            across(below, piece(below, s)).start()

        @pl.when(above < n)
        def _():
            down(t, above, piece(above, s)).wait_recv()
            if t < n - 2:
                @pl.when(z >= 1)
                def _():
                    down(t + 1, above, piece(above, s)).start()
            across(above, piece(above, s)).start()

    arrive(0)

    for j in (s, 1 - s):
        far_copy(j).wait_recv()

        @pl.loop(0, rows // tile)
        def _(i):
            at = pl.ds(pl.multiple_of(j * rows + i * tile, tile), tile)
            value = far[at, :] + p_recv[at, :]
            far[at, :] = value
            far_low[at, :] = value.astype(BF)

    for i in range(2):
        kid_copy(i).start()

    @pl.when(c == root)
    def _():
        band_own.wait()
        band_out.wait_send()

    @pl.when(c != root)
    def _():
        band_out.wait_recv()

    @pl.loop(0, n)
    def _(q):
        m_part[quarter(q), :] = lax.dot_general(
            band[:, quarter(q)],
            far_low[...],
            (((0,), (0,)), ((), ())),
            preferred_element_type=F32,
        )

    others = [lax.rem(z + d, n) for d in range(1, n)]
    for q in others:
        m_copy(q).start()
    for t in range(1, n - 2):
        arrive(t)
    for p in others:
        m_from(p).wait_recv()
    value = m_part[quarter(z), :]
    for p in others:
        value = value + m_recv[p]
    total[...] = value
    for q in others:
        g_copy(q).start()
    keep = pltpu.make_async_copy(total, summed.at[quarter(z), :], local_sem.at[6])
    keep.start()
    arrive(n - 2)

    own.wait()
    keep.wait()
    for i in range(2):
        kid_own(i).wait()
        kid_copy(i).wait_send()
        kid_copy(i).wait_recv()
    for j in (s, 1 - s):
        far_copy(j).wait_send()
    for p in others:
        m_copy(p).wait_send()
        g_copy(p).wait_send()
        g_from(p).wait_recv()
        from_peer(p).wait_recv()
        across(p, piece(p, s)).wait_send()
    across(z, sep).wait_send()
    for t in range(n - 1):
        @pl.when((z - t >= 0) & (z + 1 < n))
        def _():
            up(t, z - t, piece(z, s)).wait_send()

        @pl.when((z + t < n) & (z >= 1))
        def _():
            down(t, z + t, piece(z, s)).wait_send()


def exchange(sep, panel, side, upper):
    n = lax.axis_size("row")
    rows, strip_len = sep.shape
    w1 = panel.shape[1]
    half = w1 // 2
    kids, kid_rows, w2 = side.shape
    band_len = 2 * rows
    part = w1 // n
    any_spec = pl.BlockSpec(memory_space=pl.ANY)
    vmem = pl.BlockSpec(memory_space=pltpu.VMEM)
    dma = pltpu.SemaphoreType.DMA
    full = jax.ShapeDtypeStruct((kids, 2 * kid_rows, w2), BF)
    return pl.pallas_call(
        functools.partial(exchange_kernel, n),
        out_shape=(
            jax.ShapeDtypeStruct((n * band_len, strip_len), BF),
            jax.ShapeDtypeStruct((band_len, half), F32),
            jax.ShapeDtypeStruct((w1, half), F32),
            full,
            full,
        ),
        in_specs=[any_spec, vmem, any_spec, any_spec],
        out_specs=(any_spec, vmem, any_spec, any_spec, any_spec),
        scratch_shapes=[
            pltpu.VMEM((rows, strip_len), BF),
            pltpu.VMEM((rows, strip_len), BF),
            pltpu.VMEM((band_len, half), F32),
            pltpu.VMEM((band_len, half), F32),
            pltpu.VMEM((band_len, w1), BF),
            pltpu.VMEM((band_len, half), BF),
            pltpu.VMEM((w1, half), F32),
            pltpu.VMEM((n, part, half), F32),
            pltpu.VMEM((part, half), F32),
            dma((n,)),
            dma((n,)),
            dma((n,)),
            dma((n,)),
            dma((n,)),
            dma((2,)),
            dma((2,)),
            dma((2,)),
            dma((2,)),
            dma((2,)),
            dma((n,)),
            dma((n,)),
            dma((n,)),
            dma((n,)),
            dma((8,)),
        ],
        compiler_params=pltpu.CompilerParams(
            collective_id=0, has_side_effects=True, vmem_limit_bytes=48 * 2**20
        ),
    )(sep, panel, side, upper)


def child_kernel(blocks, *refs):
    picked = refs[:P2A]
    side, upper, near, panel, inverse, out, side_t, spread, weight, reach = refs[P2A:]
    k = pl.program_id(0)
    strip_blocks = spread.shape[0] // BLK
    first = lax.axis_index("col") * strip_blocks
    spread[...] = jnp.zeros_like(spread)
    for j in range(P2A):
        local = blocks[k, j] - first

        @pl.when((local >= 0) & (local < strip_blocks))
        def _():
            at = pl.ds(pl.multiple_of(local * BLK, BLK), BLK)
            spread[at, :] = side[0, j * BLK : (j + 1) * BLK, :]

    side_t[...] = side[0].T
    tile = 2 * BLK

    @pl.loop(0, spread.shape[0] // tile)
    def _(i):
        at = pl.ds(pl.multiple_of(i * tile, tile), tile)
        chosen = jnp.concatenate([ref[:, at] for ref in picked], axis=0)
        weight[:, at] = jnp.dot(side_t[...], chosen, preferred_element_type=F32).astype(BF)
        through = jnp.dot(panel[at, :], upper[0], preferred_element_type=F32)
        reach[at, :] = (0.5 * spread[at, :].astype(F32) - through).astype(BF)

    both = jnp.dot(weight[...], reach[...], preferred_element_type=F32)
    left_par = jnp.dot(upper[0].T, inverse[...], preferred_element_type=F32).astype(BF)
    par_term = jnp.dot(left_par, near[0], preferred_element_type=F32)
    out[0] = both + both.T + par_term


def child_terms(kid_blocks, strip, side, upper, panel, inverse):
    kids, depth, w2 = side.shape
    strip_len = strip.shape[1]
    half = inverse.shape[1]
    col_at = lax.axis_index("col")
    near = lax.dynamic_slice_in_dim(upper, col_at * half, half, 1)

    def picked_spec(j):
        return pl.BlockSpec((BLK, strip_len), lambda k, blocks: (blocks[k, j], 0))

    def kid_spec(rows):
        return pl.BlockSpec((1, rows, w2), lambda k, blocks: (k, 0, 0))

    def whole(a):
        return pl.BlockSpec(a.shape, lambda k, blocks: (0, 0))

    return pl.pallas_call(
        child_kernel,
        out_shape=jax.ShapeDtypeStruct((kids, w2, w2), F32),
        grid_spec=pltpu.PrefetchScalarGridSpec(
            num_scalar_prefetch=1,
            grid=(kids,),
            in_specs=[picked_spec(j) for j in range(P2A)]
            + [kid_spec(depth), kid_spec(depth), kid_spec(half), whole(panel), whole(inverse)],
            out_specs=kid_spec(w2),
            scratch_shapes=[
                pltpu.VMEM((w2, depth), BF),
                pltpu.VMEM((strip_len, w2), BF),
                pltpu.VMEM((w2, strip_len), BF),
                pltpu.VMEM((strip_len, w2), BF),
            ],
        ),
        compiler_params=pltpu.CompilerParams(vmem_limit_bytes=48 * 2**20),
    )(kid_blocks, *([strip] * P2A), side, upper, near, panel, inverse)


def per_device(
    sep_inverse,
    parent_panel,
    parent_pivot,
    parent_cols,
    parent_blocks,
    child_separator,
    child_parent,
    child_pivot,
    child_cols,
    child_blocks,
):
    rows_count = lax.axis_size("row")
    cols_count = lax.axis_size("col")
    subs_count = lax.axis_size("sub")
    row_at = lax.axis_index("row")
    col_at = lax.axis_index("col")
    sub_at = lax.axis_index("sub")
    strip_len = sep_inverse.shape[1]
    order = strip_len * cols_count
    band_len = order // rows_count
    w1 = parent_panel.shape[2]
    w2 = child_separator.shape[2]
    slice_one = w1 // cols_count
    slice_two = w2 // cols_count
    zero = jnp.zeros((), BF)

    count_one = lax.dynamic_index_in_dim(parent_cols, sub_at, 0, keepdims=False)
    blocks_one = lax.dynamic_index_in_dim(parent_blocks, sub_at, 0, keepdims=False)
    live_rows = jnp.broadcast_to(blocks_one[:, None] > 0, (order // BLK, BLK)).reshape(order)
    strip_live = lax.dynamic_slice_in_dim(live_rows, col_at * strip_len, strip_len, 0)
    live_one = jnp.arange(w1, dtype=jnp.int32) < count_one * BLK
    panel_one = jnp.where(strip_live[:, None] & live_one[None, :], parent_panel[0], zero)

    if rows_count == 4 and cols_count == 2 and subs_count == 2:
        whole_strip, far_rows, summed, side_rows, upper_rows = exchange(
            sep_inverse, panel_one, child_separator, child_parent
        )
        far_block = far_rows.T
    else:
        whole_strip = lax.all_gather(sep_inverse, ("row", "sub"), axis=0, tiled=True)
        own_rows = pair_gather(sep_inverse, "sub", 0)
        root_col = row_at * cols_count // rows_count
        offset = jnp.clip(row_at * band_len - root_col * strip_len, 0, strip_len - band_len)
        sent_rows = lax.dynamic_slice_in_dim(panel_one, offset, band_len, 0)
        mine_rows = spread_2(sent_rows, "col", root_col)
        far_block = pair_scatter(dot(panel_one, own_rows, ((0,), (1,))), "col", 0)
        far_round = far_block.astype(BF)
        partial_value = dot(mine_rows, far_round, ((0,), (1,)))
        summed = lax.psum(partial_value, "row")
        side_rows = pair_gather(child_separator, "col", 1)
        upper_rows = pair_gather(child_parent, "col", 1)
    keep_cols = lax.dynamic_slice_in_dim(live_one, col_at * slice_one, slice_one, 0)
    pivot_one = jnp.where(live_one[:, None] & keep_cols[None, :], parent_pivot[0], F32(0.0))
    inverse_one = pivot_one + summed
    inverse_round = inverse_one.astype(BF)

    first_kid = (row_at * subs_count + sub_at) * CHILD
    kid_cols = lax.dynamic_slice_in_dim(child_cols, first_kid, CHILD, 0)
    kid_blocks = lax.dynamic_slice_in_dim(child_blocks, first_kid, CHILD, 0)
    live_two = jnp.arange(w2, dtype=jnp.int32)[None, :] < kid_cols[:, None] * BLK
    terms = child_terms(
        kid_blocks, whole_strip, side_rows, upper_rows, panel_one, inverse_round
    )
    summed_two = pair_scatter(terms, "col", 1)
    keep_two = lax.dynamic_slice_in_dim(live_two, col_at * slice_two, slice_two, 1)
    keep_both = keep_two[:, :, None] & live_two[:, None, :]
    child_out = jnp.where(keep_both, child_pivot + summed_two, F32(0.0))
    return (inverse_one[None], (-far_block)[None], child_out)


def solution(mesh):
    return jax.shard_map(
        per_device,
        mesh=mesh,
        in_specs=(
            P(("pole", "row", "sub"), "col"),
            P(("pole", "sub"), "col", None),
            P(("pole", "sub"), None, "col"),
            P(),
            P(),
            P(("pole", "row", "sub"), "col", None),
            P(("pole", "row", "sub"), "col", None),
            P(("pole", "row", "sub"), "col", None),
            P(),
            P(),
        ),
        out_specs=(
            P(("pole", "sub"), None, "col"),
            P(("pole", "sub"), "col", "row"),
            P(("pole", "row", "sub"), "col", None),
        ),
        check_vma=False,
    )
```

```python
import functools

import jax
import jax.numpy as jnp
from jax import lax
from jax.experimental import pallas as pl
from jax.experimental.pallas import tpu as pltpu
from jax.sharding import PartitionSpec as P

BLK = 128
P2A = 8
CHILD = 2
BF = jnp.bfloat16
F32 = jnp.float32
MESH = pl.DeviceIdType.MESH


def swap(value, axis):
    return lax.ppermute(value, axis, [(0, 1), (1, 0)])


def spread_2(value, axis, source):
    kept = jnp.where(lax.axis_index(axis) == source, value, 0).astype(value.dtype)
    return lax.psum(kept, axis)


def pair_gather(value, axis, dim):
    if lax.axis_size(axis) != 2:
        return lax.all_gather(value, axis, axis=dim, tiled=True)
    other = swap(value, axis)
    first = lax.axis_index(axis) == 0
    return jnp.concatenate(
        [jnp.where(first, value, other), jnp.where(first, other, value)], axis=dim
    )


def pair_scatter(value, axis, dim):
    if lax.axis_size(axis) != 2:
        return lax.psum_scatter(value, axis, scatter_dimension=dim, tiled=True)
    half = value.shape[dim] // 2
    at = lax.axis_index(axis)
    sent = lax.dynamic_slice_in_dim(value, (1 - at) * half, half, dim)
    kept = lax.dynamic_slice_in_dim(value, at * half, half, dim)
    return kept + swap(sent, axis)


def dot(a, b, dims):
    return lax.dot_general(a, b, (dims, ((), ())), preferred_element_type=F32)


def exchange_kernel(
    n,
    sep,
    panel,
    side,
    upper,
    strip,
    far,
    summed,
    side_full,
    upper_full,
    a_own,
    a_peer,
    p_send,
    p_recv,
    band,
    far_low,
    m_part,
    m_recv,
    total,
    up_sem,
    down_sem,
    row_sem,
    sub_send,
    sub_recv,
    x_send,
    x_recv,
    band_sem,
    kid_send,
    kid_recv,
    m_send,
    m_got,
    g_send,
    g_got,
    local_sem,
):
    z = lax.axis_index("row")
    c = lax.axis_index("col")
    s = lax.axis_index("sub")
    rows = sep.shape[0]
    half = far.shape[1]
    kid_rows = side.shape[1]
    band_len = band.shape[0]
    part = m_recv.shape[1]
    sub_peer = {"sub": 1 - s}
    col_peer = {"col": 1 - c}
    root = z * 2 // n
    base = pl.multiple_of((z - root * (n // 2)) * band_len, band_len)

    barrier = pltpu.get_barrier_semaphore()
    pl.semaphore_signal(barrier, inc=1, device_id=sub_peer, device_id_type=MESH)
    pl.semaphore_signal(barrier, inc=1, device_id=col_peer, device_id_type=MESH)
    for d in range(1, n):
        pl.semaphore_signal(
            barrier, inc=1, device_id={"row": lax.rem(z + d, n)}, device_id_type=MESH
        )
    pl.semaphore_wait(barrier, n + 1)

    def piece(p, sub):
        return strip.at[pl.ds(pl.multiple_of((p * 2 + sub) * rows, rows), rows), :]

    def remote(src, dst, send, recv, to):
        return pltpu.make_async_remote_copy(
            src_ref=src, dst_ref=dst, send_sem=send, recv_sem=recv, device_id=to, device_id_type=MESH
        )

    def up(t, p, src):
        return remote(src, piece(p, s), up_sem.at[t], row_sem.at[p], {"row": z + 1})

    def down(t, p, src):
        return remote(src, piece(p, s), down_sem.at[t], row_sem.at[p], {"row": z - 1})

    def across(p, src):
        return remote(src, piece(p, s), sub_send.at[p], sub_recv.at[p], sub_peer)

    def from_peer(p):
        return remote(piece(p, 1 - s), piece(p, 1 - s), sub_send.at[p], sub_recv.at[p], sub_peer)

    def far_copy(j):
        at = pl.ds(pl.multiple_of(j * rows, rows), rows)
        return remote(p_send.at[at, :], p_recv.at[at, :], x_send.at[j], x_recv.at[j], col_peer)

    def kid_copy(i):
        src, dst = ((side, side_full), (upper, upper_full))[i]
        place = dst.at[:, pl.ds(pl.multiple_of(c * kid_rows, kid_rows), kid_rows), :]
        return remote(src, place, kid_send.at[i], kid_recv.at[i], col_peer)

    def kid_own(i):
        src, dst = ((side, side_full), (upper, upper_full))[i]
        place = dst.at[:, pl.ds(pl.multiple_of(c * kid_rows, kid_rows), kid_rows), :]
        return pltpu.make_async_copy(src, place, local_sem.at[4 + i])

    def quarter(q):
        return pl.ds(pl.multiple_of(q * part, part), part)

    low = n // 2 - 1

    def m_copy(o):
        return remote(
            m_part.at[quarter(o), :], m_recv.at[z], m_send.at[o], m_got.at[z], {"row": o + low}
        )

    def m_from(p):
        return remote(
            m_part.at[quarter(0), :], m_recv.at[p], m_send.at[0], m_got.at[p], {"row": p}
        )

    def g_copy(q):
        return remote(total, summed.at[quarter(z - low), :], g_send.at[q], g_got.at[z], {"row": q})

    def g_from(o):
        p = o + low
        return remote(total, summed.at[quarter(o), :], g_send.at[p], g_got.at[p], {"row": p})

    load = pltpu.make_async_copy(sep, a_own, local_sem.at[0])
    load.start()

    @pl.when(z + 1 < n)
    def _():
        up(0, z, sep).start()

    @pl.when(z >= 1)
    def _():
        down(0, z, sep).start()

    across(z, sep).start()
    own = pltpu.make_async_copy(sep, piece(z, s), local_sem.at[1])
    own.start()
    band_out = remote(
        panel.at[pl.ds(base, band_len), :], band, band_sem.at[0], band_sem.at[1], col_peer
    )
    band_own = pltpu.make_async_copy(panel.at[pl.ds(base, band_len), :], band, local_sem.at[2])

    @pl.when(c == root)
    def _():
        band_own.start()

    tile = min(256, rows)
    theirs = pl.ds(pl.multiple_of((1 - c) * half, half), half)
    mine = pl.ds(pl.multiple_of(c * half, half), half)

    def partial(src, dst, first, columns):
        @pl.loop(0, rows // tile)
        def _(i):
            at = pl.ds(pl.multiple_of(i * tile, tile), tile)
            to = pl.ds(pl.multiple_of(first * rows + i * tile, tile), tile)
            dst[to, :] = jnp.dot(src[at, :], panel[:, columns], preferred_element_type=F32)

    load.wait()
    partial(a_own, p_send, s, theirs)
    far_copy(s).start()

    from_peer(z).wait_recv()
    fetch = pltpu.make_async_copy(piece(z, 1 - s), a_peer, local_sem.at[3])
    fetch.start()
    fetch.wait()
    partial(a_peer, p_send, 1 - s, theirs)
    far_copy(1 - s).start()

    @pl.when(c == root)
    def _():
        band_out.start()

    for i in range(2):
        kid_own(i).start()
    partial(a_own, far, s, mine)
    partial(a_peer, far, 1 - s, mine)

    def arrive(t):
        below, above = z - 1 - t, z + 1 + t

        @pl.when(below >= 0)
        def _():
            up(t, below, piece(below, s)).wait_recv()
            if t < n - 2:
                @pl.when(z + 1 < n)
                def _():
                    up(t + 1, below, piece(below, s)).start()
            across(below, piece(below, s)).start()

        @pl.when(above < n)
        def _():
            down(t, above, piece(above, s)).wait_recv()
            if t < n - 2:
                @pl.when(z >= 1)
                def _():
                    down(t + 1, above, piece(above, s)).start()
            across(above, piece(above, s)).start()

    arrive(0)

    for j in (s, 1 - s):
        far_copy(j).wait_recv()

        @pl.loop(0, rows // tile)
        def _(i):
            at = pl.ds(pl.multiple_of(j * rows + i * tile, tile), tile)
            value = far[at, :] + p_recv[at, :]
            far[at, :] = value
            far_low[at, :] = value.astype(BF)

    for i in range(2):
        kid_copy(i).start()

    @pl.when(c == root)
    def _():
        band_own.wait()
        band_out.wait_send()

    @pl.when(c != root)
    def _():
        band_out.wait_recv()

    @pl.loop(0, band.shape[1] // tile)
    def _(q):
        at = pl.ds(pl.multiple_of(q * tile, tile), tile)
        m_part[at, :] = lax.dot_general(
            band[:, at],
            far_low[...],
            (((0,), (0,)), ((), ())),
            preferred_element_type=F32,
        )

    others = [lax.rem(z + d, n) for d in range(1, n)]
    for o in range(2):
        @pl.when(z != o + low)
        def _():
            m_copy(o).start()

    for t in range(1, n - 2):
        arrive(t)
    owner = (z == low) | (z == low + 1)

    @pl.when(owner)
    def _():
        for p in others:
            m_from(p).wait_recv()

        @pl.loop(0, part // tile)
        def _(i):
            at = pl.ds(pl.multiple_of(i * tile, tile), tile)
            mine_at = pl.ds(pl.multiple_of((z - low) * part + i * tile, tile), tile)
            value = m_part[mine_at, :]
            for p in others:
                value = value + m_recv[p, at, :]
            total[at, :] = value

        for q in others:
            g_copy(q).start()
        keep = pltpu.make_async_copy(total, summed.at[quarter(z - low), :], local_sem.at[6])
        keep.start()
        keep.wait()

    arrive(n - 2)

    own.wait()
    for i in range(2):
        kid_own(i).wait()
        kid_copy(i).wait_send()
        kid_copy(i).wait_recv()
    for j in (s, 1 - s):
        far_copy(j).wait_send()
    for p in others:
        from_peer(p).wait_recv()
        across(p, piece(p, s)).wait_send()
    across(z, sep).wait_send()
    for o in range(2):
        @pl.when(z != o + low)
        def _():
            m_copy(o).wait_send()
            g_from(o).wait_recv()

    @pl.when(owner)
    def _():
        for q in others:
            g_copy(q).wait_send()

    for t in range(n - 1):
        @pl.when((z - t >= 0) & (z + 1 < n))
        def _():
            up(t, z - t, piece(z, s)).wait_send()

        @pl.when((z + t < n) & (z >= 1))
        def _():
            down(t, z + t, piece(z, s)).wait_send()


def exchange(sep, panel, side, upper):
    n = lax.axis_size("row")
    rows, strip_len = sep.shape
    w1 = panel.shape[1]
    half = w1 // 2
    kids, kid_rows, w2 = side.shape
    band_len = 2 * rows
    part = w1 // 2
    any_spec = pl.BlockSpec(memory_space=pl.ANY)
    vmem = pl.BlockSpec(memory_space=pltpu.VMEM)
    dma = pltpu.SemaphoreType.DMA
    full = jax.ShapeDtypeStruct((kids, 2 * kid_rows, w2), BF)
    return pl.pallas_call(
        functools.partial(exchange_kernel, n),
        out_shape=(
            jax.ShapeDtypeStruct((n * band_len, strip_len), BF),
            jax.ShapeDtypeStruct((band_len, half), F32),
            jax.ShapeDtypeStruct((w1, half), F32),
            full,
            full,
        ),
        in_specs=[any_spec, vmem, any_spec, any_spec],
        out_specs=(any_spec, vmem, any_spec, any_spec, any_spec),
        scratch_shapes=[
            pltpu.VMEM((rows, strip_len), BF),
            pltpu.VMEM((rows, strip_len), BF),
            pltpu.VMEM((band_len, half), F32),
            pltpu.VMEM((band_len, half), F32),
            pltpu.VMEM((band_len, w1), BF),
            pltpu.VMEM((band_len, half), BF),
            pltpu.VMEM((w1, half), F32),
            pltpu.VMEM((n, part, half), F32),
            pltpu.VMEM((part, half), F32),
            dma((n,)),
            dma((n,)),
            dma((n,)),
            dma((n,)),
            dma((n,)),
            dma((2,)),
            dma((2,)),
            dma((2,)),
            dma((2,)),
            dma((2,)),
            dma((n,)),
            dma((n,)),
            dma((n,)),
            dma((n,)),
            dma((8,)),
        ],
        compiler_params=pltpu.CompilerParams(
            collective_id=0, has_side_effects=True, vmem_limit_bytes=48 * 2**20
        ),
    )(sep, panel, side, upper)


def child_kernel(blocks, *refs):
    picked = refs[:P2A]
    side, upper, near, panel, inverse, out, side_t, spread, weight, reach = refs[P2A:]
    k = pl.program_id(0)
    strip_blocks = spread.shape[0] // BLK
    first = lax.axis_index("col") * strip_blocks
    spread[...] = jnp.zeros_like(spread)
    for j in range(P2A):
        local = blocks[k, j] - first

        @pl.when((local >= 0) & (local < strip_blocks))
        def _():
            at = pl.ds(pl.multiple_of(local * BLK, BLK), BLK)
            spread[at, :] = side[0, j * BLK : (j + 1) * BLK, :]

    side_t[...] = side[0].T
    tile = 2 * BLK

    @pl.loop(0, spread.shape[0] // tile)
    def _(i):
        at = pl.ds(pl.multiple_of(i * tile, tile), tile)
        chosen = jnp.concatenate([ref[:, at] for ref in picked], axis=0)
        weight[:, at] = jnp.dot(side_t[...], chosen, preferred_element_type=F32).astype(BF)
        through = jnp.dot(panel[at, :], upper[0], preferred_element_type=F32)
        reach[at, :] = (0.5 * spread[at, :].astype(F32) - through).astype(BF)

    both = jnp.dot(weight[...], reach[...], preferred_element_type=F32)
    left_par = jnp.dot(upper[0].T, inverse[...], preferred_element_type=F32).astype(BF)
    par_term = jnp.dot(left_par, near[0], preferred_element_type=F32)
    out[0] = both + both.T + par_term


def child_terms(kid_blocks, strip, side, upper, panel, inverse):
    kids, depth, w2 = side.shape
    strip_len = strip.shape[1]
    half = inverse.shape[1]
    col_at = lax.axis_index("col")
    near = lax.dynamic_slice_in_dim(upper, col_at * half, half, 1)

    def picked_spec(j):
        return pl.BlockSpec((BLK, strip_len), lambda k, blocks: (blocks[k, j], 0))

    def kid_spec(rows):
        return pl.BlockSpec((1, rows, w2), lambda k, blocks: (k, 0, 0))

    def whole(a):
        return pl.BlockSpec(a.shape, lambda k, blocks: (0, 0))

    return pl.pallas_call(
        child_kernel,
        out_shape=jax.ShapeDtypeStruct((kids, w2, w2), F32),
        grid_spec=pltpu.PrefetchScalarGridSpec(
            num_scalar_prefetch=1,
            grid=(kids,),
            in_specs=[picked_spec(j) for j in range(P2A)]
            + [kid_spec(depth), kid_spec(depth), kid_spec(half), whole(panel), whole(inverse)],
            out_specs=kid_spec(w2),
            scratch_shapes=[
                pltpu.VMEM((w2, depth), BF),
                pltpu.VMEM((strip_len, w2), BF),
                pltpu.VMEM((w2, strip_len), BF),
                pltpu.VMEM((strip_len, w2), BF),
            ],
        ),
        compiler_params=pltpu.CompilerParams(vmem_limit_bytes=48 * 2**20),
    )(kid_blocks, *([strip] * P2A), side, upper, near, panel, inverse)


def per_device(
    sep_inverse,
    parent_panel,
    parent_pivot,
    parent_cols,
    parent_blocks,
    child_separator,
    child_parent,
    child_pivot,
    child_cols,
    child_blocks,
):
    rows_count = lax.axis_size("row")
    cols_count = lax.axis_size("col")
    subs_count = lax.axis_size("sub")
    row_at = lax.axis_index("row")
    col_at = lax.axis_index("col")
    sub_at = lax.axis_index("sub")
    strip_len = sep_inverse.shape[1]
    order = strip_len * cols_count
    band_len = order // rows_count
    w1 = parent_panel.shape[2]
    w2 = child_separator.shape[2]
    slice_one = w1 // cols_count
    slice_two = w2 // cols_count
    zero = jnp.zeros((), BF)

    count_one = lax.dynamic_index_in_dim(parent_cols, sub_at, 0, keepdims=False)
    blocks_one = lax.dynamic_index_in_dim(parent_blocks, sub_at, 0, keepdims=False)
    live_rows = jnp.broadcast_to(blocks_one[:, None] > 0, (order // BLK, BLK)).reshape(order)
    strip_live = lax.dynamic_slice_in_dim(live_rows, col_at * strip_len, strip_len, 0)
    live_one = jnp.arange(w1, dtype=jnp.int32) < count_one * BLK
    panel_one = jnp.where(strip_live[:, None] & live_one[None, :], parent_panel[0], zero)

    if rows_count == 4 and cols_count == 2 and subs_count == 2:
        whole_strip, far_rows, summed, side_rows, upper_rows = exchange(
            sep_inverse, panel_one, child_separator, child_parent
        )
        far_block = far_rows.T
    else:
        whole_strip = lax.all_gather(sep_inverse, ("row", "sub"), axis=0, tiled=True)
        own_rows = pair_gather(sep_inverse, "sub", 0)
        root_col = row_at * cols_count // rows_count
        offset = jnp.clip(row_at * band_len - root_col * strip_len, 0, strip_len - band_len)
        sent_rows = lax.dynamic_slice_in_dim(panel_one, offset, band_len, 0)
        mine_rows = spread_2(sent_rows, "col", root_col)
        far_block = pair_scatter(dot(panel_one, own_rows, ((0,), (1,))), "col", 0)
        far_round = far_block.astype(BF)
        partial_value = dot(mine_rows, far_round, ((0,), (1,)))
        summed = lax.psum(partial_value, "row")
        side_rows = pair_gather(child_separator, "col", 1)
        upper_rows = pair_gather(child_parent, "col", 1)
    keep_cols = lax.dynamic_slice_in_dim(live_one, col_at * slice_one, slice_one, 0)
    pivot_one = jnp.where(live_one[:, None] & keep_cols[None, :], parent_pivot[0], F32(0.0))
    inverse_one = pivot_one + summed
    inverse_round = inverse_one.astype(BF)

    first_kid = (row_at * subs_count + sub_at) * CHILD
    kid_cols = lax.dynamic_slice_in_dim(child_cols, first_kid, CHILD, 0)
    kid_blocks = lax.dynamic_slice_in_dim(child_blocks, first_kid, CHILD, 0)
    live_two = jnp.arange(w2, dtype=jnp.int32)[None, :] < kid_cols[:, None] * BLK
    terms = child_terms(
        kid_blocks, whole_strip, side_rows, upper_rows, panel_one, inverse_round
    )
    summed_two = pair_scatter(terms, "col", 1)
    keep_two = lax.dynamic_slice_in_dim(live_two, col_at * slice_two, slice_two, 1)
    keep_both = keep_two[:, :, None] & live_two[:, None, :]
    child_out = jnp.where(keep_both, child_pivot + summed_two, F32(0.0))
    return (inverse_one[None], (-far_block)[None], child_out)


def solution(mesh):
    return jax.shard_map(
        per_device,
        mesh=mesh,
        in_specs=(
            P(("pole", "row", "sub"), "col"),
            P(("pole", "sub"), "col", None),
            P(("pole", "sub"), None, "col"),
            P(),
            P(),
            P(("pole", "row", "sub"), "col", None),
            P(("pole", "row", "sub"), "col", None),
            P(("pole", "row", "sub"), "col", None),
            P(),
            P(),
        ),
        out_specs=(
            P(("pole", "sub"), None, "col"),
            P(("pole", "sub"), "col", "row"),
            P(("pole", "row", "sub"), "col", None),
        ),
        check_vma=False,
    )
```
